32 devices in a mesh: section: 8 (over y, x, core), expert: 4 (over z).
Axes of the slice: x: 2, y: 2, z: 4, core: 2. Of those that a mesh axis runs over, the one named last changes fastest.
Arguments:
- tokens: bfloat16 [8, 512, 7168], P('section', 'expert'), may hold values from -6 to 6
- cotangent: bfloat16 [8, 512, 7168], P('section', 'expert'), may hold values from -6 to 6
- expert_ids: int32 [8, 512, 8], P('section', 'expert'), may hold values from 0 to 31, as said below
- slot_index: int32 [8, 512, 8], P('section', 'expert'), may hold values from 0 to 31, as said below
- gate_scale: float32 [8, 512, 8], P('section', 'expert'), may hold values from 0.2 to 1.2
- gate_weight: bfloat16 [8, 7168, 2048], P('section', None, 'expert'), may hold values from -0.0625 to 0.0625
- up_weight: bfloat16 [8, 7168, 2048], P('section', None, 'expert'), may hold values from -0.0625 to 0.0625
- down_weight: bfloat16 [8, 2048, 7168], P('section', 'expert'), may hold values from -0.125 to 0.125
Outputs:
- next_input: bfloat16 [8, 512, 7168], P('section', 'expert')
- prior_grad: bfloat16 [8, 512, 7168], P('section', 'expert')
The draws below stay inside these ranges and needn't reach their ends.
Inputs may be any that keep to these rules, and one draw needn't show every extreme that they name: `expert_ids`: each token names 8 different experts; among the 128 tokens of one device every expert is named exactly 32 times. `slot_index`: among the routes of one device's tokens to one expert, the slots are 0 to 31, each once.
All inputs are finite; a program needn't handle non-finite values.
Results may differ from the reference program's by a relative error of at most 0.011.
Values may be sent and summed in bfloat16 or wider, within the bound.
A program may use at most 128 MiB of HBM per device.

```python
import jax
import jax.numpy as jnp
from jax import lax

D = 7168
HID = 2048
EXPERTS = 32
TOP = 8
TOK_DEV = 128
LAYERS = 8
TOKENS = 512
CAP = 32
N_EXPERT = 4


def routing_tables(key):
    blocks = LAYERS * TOKENS // TOK_DEV
    groups = TOK_DEV // EXPERTS

    def one_block(block_key):
        first, second, third, fourth = jax.random.split(block_key, 4)
        offset_keys = jax.random.split(first, groups)
        offsets = jax.vmap(lambda kk: jax.random.permutation(kk, EXPERTS)[:TOP])(offset_keys).astype(jnp.int32)
        within = jnp.arange(EXPERTS, dtype=jnp.int32)
        raw = (offsets[:, None, :] + within[None, :, None]) % EXPERTS
        raw = raw.reshape(TOK_DEV, TOP)
        relabel = jax.random.permutation(second, EXPERTS).astype(jnp.int32)
        order = jax.random.permutation(third, TOK_DEV).astype(jnp.int32)
        named = relabel[raw][order]
        score = jax.random.permutation(fourth, TOK_DEV * TOP).astype(jnp.int32)
        flat_named = named.reshape(-1)
        same = flat_named[:, None] == flat_named[None, :]
        lower = score[None, :] < score[:, None]
        slots = jnp.sum((same & lower).astype(jnp.int32), axis=1).reshape(TOK_DEV, TOP)
        return (named.astype(jnp.int32), slots.astype(jnp.int32))
    keys = jax.random.split(key, blocks)
    named, slots = lax.map(one_block, keys)
    return (named.reshape(LAYERS, TOKENS, TOP), slots.reshape(LAYERS, TOKENS, TOP))


def draw_expert_ids(key, part):
    return routing_tables(jax.random.fold_in(key, 7))[0]


def draw_slot_index(key, part):
    return routing_tables(jax.random.fold_in(key, 7))[1]


def levels(own_key, extent, cuts, least, top_value):
    def one(dim, shards_of):
        steps = jax.random.uniform(jax.random.fold_in(jax.random.fold_in(own_key, 6), dim), (shards_of,), jnp.float32, least / len(cuts), top_value / len(cuts))
        return jnp.repeat(jnp.exp(steps), extent[dim] // shards_of).reshape((-1,) + (1,) * (len(extent) - dim - 1))

    factor_of = one(*cuts[0])
    for cut in cuts[1:]:
        factor_of = factor_of * one(*cut)
    return factor_of


def scatter_about(rng, dims, spread, bound, shards=(), kind=jnp.bfloat16):
    result = spread * jax.random.normal(rng, dims, jnp.float32)
    if shards:
        result = result * levels(rng, dims, shards, -0.22, 0.18)
    return jnp.clip(result, -bound, bound).astype(kind)


def setup_inputs(seed: int = 0) -> dict:
    splits = jax.random.split(jax.random.key(seed), 9)
    tokens = scatter_about(splits[0], (LAYERS, TOKENS, D), 1.0, 6.0, ((0, 8), (1, 4)))
    cotangent = scatter_about(splits[1], (LAYERS, TOKENS, D), 1.0, 6.0, ((0, 8), (1, 4)))
    expert_ids = draw_expert_ids(jax.random.fold_in(splits[8], 71), 0)
    slot_index = draw_slot_index(jax.random.fold_in(splits[8], 71), 0)
    gate_scale = jnp.clip(0.2 + 1 * jax.random.uniform(splits[4], (LAYERS, TOKENS, TOP), jnp.float32) ** levels(splits[4], (LAYERS, TOKENS, TOP), ((0, 8), (1, 4)), -0.2, 0.2), 0.2, 1.2)
    gate_weight = scatter_about(splits[5], (LAYERS, D, HID), D ** -0.5, 0.0625, ((0, 8), (2, 4)))
    up_weight = scatter_about(splits[6], (LAYERS, D, HID), D ** -0.5, 0.0625, ((0, 8), (2, 4)))
    down_weight = scatter_about(splits[7], (LAYERS, HID, D), HID ** -0.5, 0.125, ((0, 8), (1, 4)))
    return dict(tokens=tokens, cotangent=cotangent, expert_ids=expert_ids, slot_index=slot_index, gate_scale=gate_scale, gate_weight=gate_weight, up_weight=up_weight, down_weight=down_weight)


def silu_parts(gate):
    sig = jax.nn.sigmoid(gate)
    return gate * sig, sig * (1.0 + gate * (1.0 - sig))


def rounded(value):
    return lax.optimization_barrier(value.astype(jnp.bfloat16)).astype(jnp.float32)


def one_section(section, tokens, cotangent, ids, slots, scale, gate_w, up_w, down_w):
    rows_all = CAP * N_EXPERT
    hit = ids == section
    chosen = jnp.any(hit, axis=1)
    slot = jnp.sum(jnp.where(hit, slots, 0), axis=1).astype(jnp.int32)
    weight = jnp.sum(jnp.where(hit, scale, jnp.float32(0.0)), axis=1)
    block = jnp.arange(tokens.shape[0], dtype=jnp.int32) // TOK_DEV
    place = (block * CAP + slot).astype(jnp.int32)
    dest = jnp.where(chosen, place, rows_all).astype(jnp.int32)
    sent = jnp.zeros((rows_all, D), jnp.bfloat16).at[dest].set(tokens, mode="drop")
    carried = (weight[:, None] * cotangent.astype(jnp.float32)).astype(jnp.bfloat16)
    back = jnp.zeros((rows_all, D), jnp.bfloat16).at[dest].set(carried, mode="drop")
    gate = jnp.dot(sent, gate_w, preferred_element_type=jnp.float32)
    up = jnp.dot(sent, up_w, preferred_element_type=jnp.float32)
    act, slope = silu_parts(gate)
    hidden = (act * up).astype(jnp.bfloat16)
    grad_hidden = jnp.dot(back, down_w.T, preferred_element_type=jnp.float32)
    grad_up = (grad_hidden * act).astype(jnp.bfloat16)
    grad_gate = (grad_hidden * up * slope).astype(jnp.bfloat16)
    width = HID // N_EXPERT

    def add_share(carry, index):
        start = (index * width).astype(jnp.int32)
        hid_part = lax.dynamic_slice_in_dim(hidden, start, width, 1)
        down_part = lax.dynamic_slice_in_dim(down_w, start, width, 0)
        gate_part = lax.dynamic_slice_in_dim(gate_w, start, width, 1)
        up_part = lax.dynamic_slice_in_dim(up_w, start, width, 1)
        gg_part = lax.dynamic_slice_in_dim(grad_gate, start, width, 1)
        gu_part = lax.dynamic_slice_in_dim(grad_up, start, width, 1)
        ahead = jnp.dot(hid_part, down_part, preferred_element_type=jnp.float32)
        behind = jnp.dot(gg_part, gate_part.T, preferred_element_type=jnp.float32)
        behind = behind + jnp.dot(gu_part, up_part.T, preferred_element_type=jnp.float32)
        return (carry[0] + rounded(ahead), carry[1] + rounded(behind)), None

    zeros = jnp.zeros((rows_all, D), jnp.float32)
    (combined, inward), _ = lax.scan(add_share, (zeros, zeros), jnp.arange(N_EXPERT, dtype=jnp.int32))
    output = tokens.astype(jnp.float32) + weight[:, None] * combined[place]
    grad_in = cotangent.astype(jnp.float32) + jnp.where(chosen[:, None], inward[place], jnp.float32(0.0))
    return output.astype(jnp.bfloat16), grad_in.astype(jnp.bfloat16)


def reference(tokens, cotangent, expert_ids, slot_index, gate_scale, gate_weight, up_weight, down_weight):
    ahead_list = []
    behind_list = []
    for section in range(LAYERS):
        output, grad_in = one_section(section, tokens[section], cotangent[section], expert_ids[section], slot_index[section], gate_scale[section], gate_weight[section], up_weight[section], down_weight[section])
        ahead_list.append(output)
        behind_list.append(grad_in)
    ahead = jnp.stack(ahead_list)
    behind = jnp.stack(behind_list)
    next_input = jnp.concatenate([jnp.zeros_like(ahead[:1]), ahead[:-1]], axis=0)
    prior_grad = jnp.concatenate([behind[1:], jnp.zeros_like(behind[:1])], axis=0)
    return next_input, prior_grad
```

```python
import functools

import jax
import jax.numpy as jnp
from jax import lax
from jax.experimental import pallas as pl
from jax.experimental.pallas import tpu as pltpu
from jax.sharding import PartitionSpec as P

CAP = 32
CH = 1024
PIECES = 2
MESH = pl.DeviceIdType.MESH
NT = (((1,), (1,)), ((), ()))
TN = (((0,), (0,)), ((), ()))


def kernel(
    n,
    n_sec,
    ids_ref,
    slots_ref,
    scale_ref,
    tok_hbm,
    cot_hbm,
    gw_hbm,
    uw_hbm,
    dw_hbm,
    next_hbm,
    prior_hbm,
    tok,
    cot,
    gw,
    uw,
    dw,
    gs,
    gb,
    rs_in,
    fin,
    shift,
    route,
    route_in,
    gate,
    up,
    hid,
    load_sem,
    ag_send,
    ag_recv,
    rs_send,
    rs_recv,
    fin_send,
    fin_recv,
    shift_send,
    shift_recv,
    route_send,
    route_recv,
    out_sem,
):
    f32, bf16 = jnp.float32, jnp.bfloat16
    sec = lax.axis_index("section")
    me = lax.axis_index("expert")
    d = tok.shape[1]
    nc = d // CH
    pw = d // PIECES
    has_right, has_left = me < n - 1, me > 0
    has_next, has_prev = sec < n_sec - 1, sec > 0
    right = (sec, jnp.minimum(me + 1, n - 1))
    left = (sec, jnp.maximum(me - 1, 0))
    after = (jnp.minimum(sec + 1, n_sec - 1), me)
    before = (jnp.maximum(sec - 1, 0), me)
    neighbours = ((has_right, right), (has_left, left), (has_next, after), (has_prev, before))
    bufs = (gs, gb)

    loads = [
        pltpu.make_async_copy(src, dst, load_sem.at[k])
        for k, (src, dst) in enumerate(
            ((tok_hbm, tok), (cot_hbm, cot), (gw_hbm, gw), (uw_hbm, uw), (dw_hbm, dw))
        )
    ]
    for load in loads:
        load.start()

    barrier = pltpu.get_barrier_semaphore()
    for exists, where in neighbours:

        @pl.when(exists)
        def _():
            pl.semaphore_signal(barrier, inc=1, device_id=where, device_id_type=MESH)

    def col(c):
        return pl.ds(pl.multiple_of(c * CH, CH), CH)

    hit = ids_ref[...] == sec
    slot = jnp.sum(jnp.where(hit, slots_ref[...], 0), axis=1, keepdims=True)
    weight = jnp.sum(jnp.where(hit, scale_ref[...], 0.0), axis=1, keepdims=True)
    chosen = jnp.sum(hit.astype(jnp.int32), axis=1, keepdims=True)
    lane = lax.broadcasted_iota(jnp.int32, (hit.shape[0], 128), 1)
    picks = jnp.where((lane == slot) & (chosen > 0), 1.0, 0.0)
    route[...] = jnp.where(lane < CAP, picks, weight)

    def gather_own(a):
        @pl.loop(0, nc)
        def _(c):
            table = route[:, :CAP].astype(bf16)
            if a == 0:
                rows = tok[:, col(c)]
            else:
                rows = (route[:, CAP : CAP + 1] * cot[:, col(c)].astype(f32)).astype(bf16)
            got = lax.dot_general(table, rows, TN, preferred_element_type=f32)
            bufs[a][me, :, col(c)] = got.astype(bf16)

    def ag_copy(a, j, p, way):
        ref = bufs[a].at[j, :, pl.ds(p * pw, pw)]
        return pltpu.make_async_remote_copy(
            src_ref=ref,
            dst_ref=ref,
            send_sem=ag_send.at[a, way, j, p],
            recv_sem=ag_recv.at[a, j, p],
            device_id=(right, left)[way],
            device_id_type=MESH,
        )

    def ag_step(a, s):
        for way, j, ok in ((0, me - s, me - s >= 0), (1, me + s, me + s < n)):
            for p in range(PIECES):

                @pl.when(ok)
                def _():
                    if s > 0:
                        ag_copy(a, j, p, way).wait_recv()
                    if s < n - 1:

                        @pl.when((has_right, has_left)[way])
                        def _():
                            ag_copy(a, j, p, way).start()

    def ag_sent(a):
        for s in range(n - 1):
            for way, j, ok in ((0, me - s, me - s >= 0), (1, me + s, me + s < n)):

                @pl.when(ok & (has_right, has_left)[way])
                def _():
                    for p in range(PIECES):
                        ag_copy(a, j, p, way).wait_send()

    def rs_copy(a, j, c, way):
        into = j if way == 0 else jnp.where(j == me - 1, n, j)
        return pltpu.make_async_remote_copy(
            src_ref=bufs[a].at[j, :, col(c)],
            dst_ref=rs_in.at[a, into, :, col(c)],
            send_sem=rs_send.at[a, j, c],
            recv_sem=rs_recv.at[a, into, c],
            device_id=(right, left)[way],
            device_id_type=MESH,
        )

    def rs_take(a, j, into, c):
        pltpu.make_async_remote_copy(
            src_ref=bufs[a].at[j, :, col(c)],
            dst_ref=rs_in.at[a, into, :, col(c)],
            send_sem=rs_send.at[a, j, c],
            recv_sem=rs_recv.at[a, into, c],
            device_id=right,
            device_id_type=MESH,
        ).wait_recv()
        total = bufs[a][j, :, col(c)].astype(f32) + rs_in[a, into, :, col(c)].astype(f32)
        bufs[a][j, :, col(c)] = total.astype(bf16)

    def rs_first(a, c):
        for s in range(n - 1):

            @pl.when(me == 0)
            def _():
                rs_copy(a, n - 1 - s, c, 0).start()

            @pl.when(me == n - 1)
            def _():
                rs_copy(a, s, c, 1).start()

    def fin_copy(a, c):
        return pltpu.make_async_remote_copy(
            src_ref=bufs[a].at[me, :, col(c)],
            dst_ref=fin.at[a, :, col(c)],
            send_sem=fin_send.at[a, c],
            recv_sem=fin_recv.at[a, c],
            device_id=(after, before)[a],
            device_id_type=MESH,
        )

    def rs_relay(a, c):
        for s in range(n - 1):
            for way, j, ok in (
                (0, n - 1 - s, (n - 1 - s > me) & has_left),
                (1, s, (s < me) & has_right),
            ):

                @pl.when(ok)
                def _():
                    rs_take(a, j, j, c)
                    rs_copy(a, j, c, way).start()

        @pl.when(has_left)
        def _():
            rs_take(a, me, me, c)

        @pl.when(has_right)
        def _():
            rs_take(a, me, n, c)

        @pl.when((has_next, has_prev)[a])
        def _():
            fin_copy(a, c).start()

    def rs_sent(a, c):
        for j in range(n):
            for way, ok in ((0, j > me), (1, j < me)):

                @pl.when(ok)
                def _():
                    rs_copy(a, j, c, way).wait_send()

        @pl.when((has_next, has_prev)[a])
        def _():
            fin_copy(a, c).wait_send()

    def shift_copy(a):
        return pltpu.make_async_remote_copy(
            src_ref=(tok, cot)[a],
            dst_ref=shift.at[a],
            send_sem=shift_send.at[a],
            recv_sem=shift_recv.at[a],
            device_id=(after, before)[a],
            device_id_type=MESH,
        )

    def route_copy(a):
        return pltpu.make_async_remote_copy(
            src_ref=route,
            dst_ref=route_in.at[a],
            send_sem=route_send.at[a],
            recv_sem=route_recv.at[a],
            device_id=(after, before)[a],
            device_id_type=MESH,
        )

    def out_copy(a, c):
        return pltpu.make_async_copy(
            shift.at[a, :, col(c)], (next_hbm, prior_hbm)[a].at[:, col(c)], out_sem.at[a, c]
        )

    sends_on = (has_next, has_prev)
    takes_from = (has_prev, has_next)

    def finish(a, c):
        @pl.when(takes_from[a])
        def _():
            fin_copy(a, c).wait_recv()
            table = route_in[a, :, :CAP].astype(bf16)
            rows = jnp.dot(table, fin[a, :, col(c)], preferred_element_type=f32)
            if a == 0:
                rows = route_in[a, :, CAP : CAP + 1] * rows
            shift[a, :, col(c)] = (shift[a, :, col(c)].astype(f32) + rows).astype(bf16)

        @pl.when(jnp.logical_not(takes_from[a]))
        def _():
            shift[a, :, col(c)] = jnp.zeros((shift.shape[1], CH), bf16)

        out_copy(a, c).start()

    loads[0].wait()
    gather_own(0)
    peers = sum(exists.astype(jnp.int32) for exists, _w in neighbours)
    pl.semaphore_wait(barrier, peers)

    ag_step(0, 0)
    loads[1].wait()
    gather_own(1)
    for a in range(2):

        @pl.when(sends_on[a])
        def _():
            route_copy(a).start()
            shift_copy(a).start()

    for s in range(n):
        if s > 0:
            ag_step(0, s)
        for p in range(PIECES):

            @pl.when((me == s) & has_right)
            def _():
                ag_copy(1, me, p, 0).start()

            @pl.when((me == n - 1 - s) & has_left)
            def _():
                ag_copy(1, me, p, 1).start()

    loads[2].wait()
    loads[3].wait()
    m = n * CAP
    gate[...] = jnp.zeros_like(gate)
    up[...] = jnp.zeros_like(up)

    @pl.loop(0, nc)
    def _(c):
        rows = gs[:, :, col(c)].reshape(m, CH)
        gate[...] += jnp.dot(rows, gw[col(c), :], preferred_element_type=f32)
        up[...] += jnp.dot(rows, uw[col(c), :], preferred_element_type=f32)

    g = gate[...]
    hid[0] = (g * jax.nn.sigmoid(g) * up[...]).astype(bf16)
    loads[4].wait()
    ag_sent(0)

    @pl.loop(0, nc)
    def _(c):
        part = jnp.dot(hid[0], dw[:, col(c)], preferred_element_type=f32)
        gs[:, :, col(c)] = part.astype(bf16).reshape(n, CAP, CH)
        rs_first(0, c)

    for s in range(1, n):
        ag_step(1, s)

    def grad_hidden(c, total):
        rows = gb[:, :, col(c)].reshape(m, CH)
        return total + lax.dot_general(rows, dw[:, col(c)], NT, preferred_element_type=f32)

    gh = lax.fori_loop(0, nc, grad_hidden, jnp.zeros(gate.shape, f32))
    g = gate[...]
    sig = jax.nn.sigmoid(g)
    hid[0] = (gh * (g * sig)).astype(bf16)
    hid[1] = (gh * up[...] * (sig * (1.0 + g * (1.0 - sig)))).astype(bf16)
    ag_sent(1)

    @pl.loop(0, nc)
    def _(c):
        rs_relay(0, c)

    @pl.loop(0, nc)
    def _(c):
        part = lax.dot_general(hid[1], gw[col(c), :], NT, preferred_element_type=f32)
        part += lax.dot_general(hid[0], uw[col(c), :], NT, preferred_element_type=f32)
        gb[:, :, col(c)] = part.astype(bf16).reshape(n, CAP, CH)
        rs_first(1, c)

    for a in range(2):

        @pl.when(takes_from[a])
        def _():
            route_copy(a).wait_recv()
            shift_copy(a).wait_recv()

    @pl.loop(0, nc)
    def _(c):
        rs_relay(1, c)
        finish(0, c)

    @pl.loop(0, nc)
    def _(c):
        finish(1, c)

    for a in range(2):

        @pl.when(sends_on[a])
        def _():
            route_copy(a).wait_send()
            shift_copy(a).wait_send()

    @pl.loop(0, nc)
    def _(c):
        for a in range(2):
            rs_sent(a, c)
            out_copy(a, c).wait()


def body(
    n, n_sec, tokens, cotangent, expert_ids, slot_index, gate_scale, gate_weight, up_weight, down_weight
):
    t, d = tokens.shape[1:]
    h = gate_weight.shape[2]
    nc = d // CH
    m = n * CAP
    bf16, f32 = jnp.bfloat16, jnp.float32
    dma = pltpu.SemaphoreType.DMA
    vmem = pl.BlockSpec(memory_space=pltpu.VMEM)
    hbm = pl.BlockSpec(memory_space=pl.ANY)
    nxt, prior = pl.pallas_call(
        functools.partial(kernel, n, n_sec),
        out_shape=(jax.ShapeDtypeStruct((t, d), bf16), jax.ShapeDtypeStruct((t, d), bf16)),
        in_specs=[vmem] * 3 + [hbm] * 5,
        out_specs=(hbm, hbm),
        scratch_shapes=[
            pltpu.VMEM((t, d), bf16),
            pltpu.VMEM((t, d), bf16),
            pltpu.VMEM((d, h), bf16),
            pltpu.VMEM((d, h), bf16),
            pltpu.VMEM((h, d), bf16),
            pltpu.VMEM((n, CAP, d), bf16),
            pltpu.VMEM((n, CAP, d), bf16),
            pltpu.VMEM((2, n + 1, CAP, d), bf16),
            pltpu.VMEM((2, CAP, d), bf16),
            pltpu.VMEM((2, t, d), bf16),
            pltpu.VMEM((t, 128), f32),
            pltpu.VMEM((2, t, 128), f32),
            pltpu.VMEM((m, h), f32),
            pltpu.VMEM((m, h), f32),
            pltpu.VMEM((2, m, h), bf16),
            dma((5,)),
            dma((2, 2, n, PIECES)),
            dma((2, n, PIECES)),
            dma((2, n, nc)),
            dma((2, n + 1, nc)),
            dma((2, nc)),
            dma((2, nc)),
            dma((2,)),
            dma((2,)),
            dma((2,)),
            dma((2,)),
            dma((2, nc)),
        ],
        compiler_params=pltpu.CompilerParams(
            collective_id=0, has_side_effects=True, vmem_limit_bytes=58 * 1024 * 1024
        ),
        cost_estimate=pl.CostEstimate(
            flops=12 * m * d * h, bytes_accessed=6 * d * h + 8 * t * d, transcendentals=0
        ),
    )(
        expert_ids[0],
        slot_index[0],
        gate_scale[0],
        tokens[0],
        cotangent[0],
        gate_weight[0],
        up_weight[0],
        down_weight[0],
    )
    return nxt[None], prior[None]


def solution(mesh):
    rows = P("section", "expert", None)
    in_specs = (rows,) * 5 + (P("section", None, "expert"),) * 2 + (rows,)
    return jax.shard_map(
        functools.partial(body, mesh.shape["expert"], mesh.shape["section"]),
        mesh=mesh,
        in_specs=in_specs,
        out_specs=(rows, rows),
        check_vma=False,
    )
```

```python
import functools

import jax
import jax.numpy as jnp
from jax import lax
from jax.experimental import pallas as pl
from jax.experimental.pallas import tpu as pltpu
from jax.sharding import PartitionSpec as P

CAP = 32
CH = 1024
AHEAD = 2
MESH = pl.DeviceIdType.MESH
NT = (((1,), (1,)), ((), ()))
TN = (((0,), (0,)), ((), ()))


def kernel(
    n,
    n_sec,
    ids_ref,
    slots_ref,
    scale_ref,
    tok_hbm,
    cot_hbm,
    gw_hbm,
    uw_hbm,
    dw_hbm,
    next_hbm,
    prior_hbm,
    tok,
    cot,
    gw,
    uw,
    dw,
    rows_all,
    rs_in,
    fin,
    shift,
    route,
    route_in,
    gate,
    up,
    grad,
    hid,
    load_sem,
    ag_send,
    ag_recv,
    rs_send,
    rs_recv,
    fin_send,
    fin_recv,
    shift_send,
    shift_recv,
    route_send,
    route_recv,
    out_sem,
):
    f32, bf16 = jnp.float32, jnp.bfloat16
    sec = lax.axis_index("section")
    me = lax.axis_index("expert")
    d = tok.shape[1]
    nc = d // CH
    has_right, has_left = me < n - 1, me > 0
    has_next, has_prev = sec < n_sec - 1, sec > 0
    right = (sec, jnp.minimum(me + 1, n - 1))
    left = (sec, jnp.maximum(me - 1, 0))
    after = (jnp.minimum(sec + 1, n_sec - 1), me)
    before = (jnp.maximum(sec - 1, 0), me)
    neighbours = ((has_right, right), (has_left, left), (has_next, after), (has_prev, before))

    loads = [
        pltpu.make_async_copy(src, dst, load_sem.at[k])
        for k, (src, dst) in enumerate(
            ((tok_hbm, tok), (cot_hbm, cot), (gw_hbm, gw), (uw_hbm, uw), (dw_hbm, dw))
        )
    ]
    for load in loads:
        load.start()

    barrier = pltpu.get_barrier_semaphore()
    for exists, where in neighbours:

        @pl.when(exists)
        def _():
            pl.semaphore_signal(barrier, inc=1, device_id=where, device_id_type=MESH)

    def col(c):
        return pl.ds(pl.multiple_of(c * CH, CH), CH)

    hit = ids_ref[...] == sec
    slot = jnp.sum(jnp.where(hit, slots_ref[...], 0), axis=0, keepdims=True)
    weight = jnp.sum(jnp.where(hit, scale_ref[...], 0.0), axis=0, keepdims=True)
    chosen = jnp.sum(hit.astype(jnp.int32), axis=0, keepdims=True)
    place = lax.broadcasted_iota(jnp.int32, (128, hit.shape[1]), 0)
    picks = jnp.where((place == slot) & (chosen > 0), 1.0, 0.0)
    route[...] = jnp.transpose(jnp.where(place < CAP, picks, weight))

    def gather_own(a):
        @pl.loop(0, nc)
        def _(c):
            table = route[:, :CAP].astype(bf16)
            if a == 0:
                rows = tok[:, col(c)]
            else:
                rows = (route[:, CAP : CAP + 1] * cot[:, col(c)].astype(f32)).astype(bf16)
            got = lax.dot_general(table, rows, TN, preferred_element_type=f32)
            rows_all[a, me, :, col(c)] = got.astype(bf16)

    def ag_copy(u, j, way):
        ref = rows_all.at[u // nc, j, :, col(u % nc)]
        return pltpu.make_async_remote_copy(
            src_ref=ref,
            dst_ref=ref,
            send_sem=ag_send.at[u, way, j],
            recv_sem=ag_recv.at[u, j],
            device_id=(right, left)[way],
            device_id_type=MESH,
        )

    def ag_own(u):
        for way in range(2):

            @pl.when((has_right, has_left)[way])
            def _():
                ag_copy(u, me, way).start()

    def ag_step(u, s):
        for way, j, ok in ((0, me - s, me - s >= 0), (1, me + s, me + s < n)):

            @pl.when(ok)
            def _():
                ag_copy(u, j, way).wait_recv()
                if s < n - 1:

                    @pl.when((has_right, has_left)[way])
                    def _():
                        ag_copy(u, j, way).start()

    def ag_sent(u):
        for s in range(n - 1):
            for way, j, ok in ((0, me - s, me - s >= 0), (1, me + s, me + s < n)):

                @pl.when(ok & (has_right, has_left)[way])
                def _():
                    ag_copy(u, j, way).wait_send()

    def rs_copy(a, j, c, way):
        into = j if way == 0 else jnp.where(j == me - 1, n, j)
        return pltpu.make_async_remote_copy(
            src_ref=rows_all.at[a, j, :, col(c)],
            dst_ref=rs_in.at[a, into, :, col(c)],
            send_sem=rs_send.at[a, j, c],
            recv_sem=rs_recv.at[a, into, c],
            device_id=(right, left)[way],
            device_id_type=MESH,
        )

    def rs_take(a, j, into, c):
        pltpu.make_async_remote_copy(
            src_ref=rows_all.at[a, j, :, col(c)],
            dst_ref=rs_in.at[a, into, :, col(c)],
            send_sem=rs_send.at[a, j, c],
            recv_sem=rs_recv.at[a, into, c],
            device_id=right,
            device_id_type=MESH,
        ).wait_recv()
        total = rows_all[a, j, :, col(c)].astype(f32) + rs_in[a, into, :, col(c)].astype(f32)
        rows_all[a, j, :, col(c)] = total.astype(bf16)

    def fin_copy(a, c):
        return pltpu.make_async_remote_copy(
            src_ref=rows_all.at[a, me, :, col(c)],
            dst_ref=fin.at[a, :, col(c)],
            send_sem=fin_send.at[a, c],
            recv_sem=fin_recv.at[a, c],
            device_id=(after, before)[a],
            device_id_type=MESH,
        )

    def rs_step(a, b):
        for way in range(2):
            c = b - (me, n - 1 - me)[way]
            into = (me, n)[way]
            has_in = (has_left, has_right)[way]

            @pl.when((c >= 0) & (c < nc))
            def _():
                for s in range(n - 1):
                    j = (n - 1 - s, s)[way]

                    @pl.when((j > me, j < me)[way])
                    def _():
                        @pl.when(has_in)
                        def _():
                            rs_take(a, j, j, c)

                        rs_copy(a, j, c, way).start()

                @pl.when(has_in)
                def _():
                    rs_take(a, me, into, c)

        c = b - (n - 1)

        @pl.when((c >= 0) & (c < nc) & (has_next, has_prev)[a])
        def _():
            fin_copy(a, c).start()

    def rs_sent(a, c):
        for j in range(n):
            for way, ok in ((0, j > me), (1, j < me)):

                @pl.when(ok)
                def _():
                    rs_copy(a, j, c, way).wait_send()

        @pl.when((has_next, has_prev)[a])
        def _():
            fin_copy(a, c).wait_send()

    def shift_copy(a):
        return pltpu.make_async_remote_copy(
            src_ref=(tok, cot)[a],
            dst_ref=shift.at[a],
            send_sem=shift_send.at[a],
            recv_sem=shift_recv.at[a],
            device_id=(after, before)[a],
            device_id_type=MESH,
        )

    def route_copy(a):
        return pltpu.make_async_remote_copy(
            src_ref=route,
            dst_ref=route_in.at[a],
            send_sem=route_send.at[a],
            recv_sem=route_recv.at[a],
            device_id=(after, before)[a],
            device_id_type=MESH,
        )

    def out_copy(a, c):
        return pltpu.make_async_copy(
            shift.at[a, :, col(c)], (next_hbm, prior_hbm)[a].at[:, col(c)], out_sem.at[a, c]
        )

    sends_on = (has_next, has_prev)
    takes_from = (has_prev, has_next)

    def finish(a, c):
        @pl.when(takes_from[a])
        def _():
            fin_copy(a, c).wait_recv()
            table = route_in[a, :, :CAP].astype(bf16)
            rows = jnp.dot(table, fin[a, :, col(c)], preferred_element_type=f32)
            if a == 0:
                rows = route_in[a, :, CAP : CAP + 1] * rows
            shift[a, :, col(c)] = (shift[a, :, col(c)].astype(f32) + rows).astype(bf16)

        @pl.when(jnp.logical_not(takes_from[a]))
        def _():
            shift[a, :, col(c)] = jnp.zeros((shift.shape[1], CH), bf16)

        out_copy(a, c).start()

    loads[0].wait()
    gather_own(0)
    peers = sum(exists.astype(jnp.int32) for exists, _w in neighbours)
    pl.semaphore_wait(barrier, peers)

    for u in range(AHEAD):
        ag_own(u)
    loads[1].wait()
    gather_own(1)
    for a in range(2):

        @pl.when(sends_on[a])
        def _():
            route_copy(a).start()
            shift_copy(a).start()

    m = n * CAP
    gate[...] = jnp.zeros_like(gate)
    up[...] = jnp.zeros_like(up)
    grad[...] = jnp.zeros_like(grad)

    @pl.loop(0, 2 * nc + n - 1)
    def _(t):
        @pl.when(t + AHEAD < 2 * nc)
        def _():
            ag_own(t + AHEAD)

        for s in range(1, n):

            @pl.when((t >= s) & (t - s < 2 * nc))
            def _():
                ag_step(t - s, s)

        c = t - (n - 1)
        b = c - nc

        @pl.when(c == 0)
        def _():
            loads[2].wait()
            loads[3].wait()

        @pl.when((c >= 0) & (b < 0))
        def _():
            rows = rows_all[0, :, :, col(c)].reshape(m, CH)
            gate[...] += jnp.dot(rows, gw[col(c), :], preferred_element_type=f32)
            up[...] += jnp.dot(rows, uw[col(c), :], preferred_element_type=f32)

        @pl.when(b == 0)
        def _():
            g = gate[...]
            hid[0] = (g * jax.nn.sigmoid(g) * up[...]).astype(bf16)
            loads[4].wait()

        @pl.when(b >= 0)
        def _():
            ag_sent(b)
            part = jnp.dot(hid[0], dw[:, col(b)], preferred_element_type=f32)
            rows_all[0, :, :, col(b)] = part.astype(bf16).reshape(n, CAP, CH)
            rs_step(0, b)
            rows = rows_all[1, :, :, col(b)].reshape(m, CH)
            grad[...] += lax.dot_general(rows, dw[:, col(b)], NT, preferred_element_type=f32)

    g = gate[...]
    sig = jax.nn.sigmoid(g)
    hid[0] = (grad[...] * (g * sig)).astype(bf16)
    hid[1] = (grad[...] * up[...] * (sig * (1.0 + g * (1.0 - sig)))).astype(bf16)

    for a in range(2):

        @pl.when(takes_from[a])
        def _():
            route_copy(a).wait_recv()
            shift_copy(a).wait_recv()

    @pl.loop(0, nc + n)
    def _(b):
        @pl.when(b < nc)
        def _():
            ag_sent(nc + b)
            part = lax.dot_general(hid[1], gw[col(b), :], NT, preferred_element_type=f32)
            part += lax.dot_general(hid[0], uw[col(b), :], NT, preferred_element_type=f32)
            rows_all[1, :, :, col(b)] = part.astype(bf16).reshape(n, CAP, CH)

        rs_step(0, nc + b)
        rs_step(1, b)

        @pl.when(b < nc)
        def _():
            finish(0, b)

        @pl.when(b >= n)
        def _():
            finish(1, b - n)

    for a in range(2):

        @pl.when(sends_on[a])
        def _():
            route_copy(a).wait_send()
            shift_copy(a).wait_send()

    @pl.loop(0, nc)
    def _(c):
        for a in range(2):
            rs_sent(a, c)
            out_copy(a, c).wait()


def body(
    n, n_sec, tokens, cotangent, expert_ids, slot_index, gate_scale, gate_weight, up_weight, down_weight
):
    t, d = tokens.shape[1:]
    h = gate_weight.shape[2]
    nc = d // CH
    m = n * CAP
    bf16, f32 = jnp.bfloat16, jnp.float32
    dma = pltpu.SemaphoreType.DMA
    vmem = pl.BlockSpec(memory_space=pltpu.VMEM)
    hbm = pl.BlockSpec(memory_space=pl.ANY)
    nxt, prior = pl.pallas_call(
        functools.partial(kernel, n, n_sec),
        out_shape=(jax.ShapeDtypeStruct((t, d), bf16), jax.ShapeDtypeStruct((t, d), bf16)),
        in_specs=[vmem] * 3 + [hbm] * 5,
        out_specs=(hbm, hbm),
        scratch_shapes=[
            pltpu.VMEM((t, d), bf16),
            pltpu.VMEM((t, d), bf16),
            pltpu.VMEM((d, h), bf16),
            pltpu.VMEM((d, h), bf16),
            pltpu.VMEM((h, d), bf16),
            pltpu.VMEM((2, n, CAP, d), bf16),
            pltpu.VMEM((2, n + 1, CAP, d), bf16),
            pltpu.VMEM((2, CAP, d), bf16),
            pltpu.VMEM((2, t, d), bf16),
            pltpu.VMEM((t, 128), f32),
            pltpu.VMEM((2, t, 128), f32),
            pltpu.VMEM((m, h), f32),
            pltpu.VMEM((m, h), f32),
            pltpu.VMEM((m, h), f32),
            pltpu.VMEM((2, m, h), bf16),
            dma((5,)),
            dma((2 * nc, 2, n)),
            dma((2 * nc, n)),
            dma((2, n, nc)),
            dma((2, n + 1, nc)),
            dma((2, nc)),
            dma((2, nc)),
            dma((2,)),
            dma((2,)),
            dma((2,)),
            dma((2,)),
            dma((2, nc)),
        ],
        compiler_params=pltpu.CompilerParams(
            collective_id=0, has_side_effects=True, vmem_limit_bytes=58 * 1024 * 1024
        ),
        cost_estimate=pl.CostEstimate(
            flops=12 * m * d * h, bytes_accessed=6 * d * h + 8 * t * d, transcendentals=0
        ),
    )(
        expert_ids[0].T,
        slot_index[0].T,
        gate_scale[0].T,
        tokens[0],
        cotangent[0],
        gate_weight[0],
        up_weight[0],
        down_weight[0],
    )
    return nxt[None], prior[None]


def solution(mesh):
    rows = P("section", "expert", None)
    in_specs = (rows,) * 5 + (P("section", None, "expert"),) * 2 + (rows,)
    return jax.shard_map(
        functools.partial(body, mesh.shape["expert"], mesh.shape["section"]),
        mesh=mesh,
        in_specs=in_specs,
        out_specs=(rows, rows),
        check_vma=False,
    )
```

```python
import functools

import jax
import jax.numpy as jnp
from jax import lax
from jax.experimental import pallas as pl
from jax.experimental.pallas import tpu as pltpu
from jax.sharding import PartitionSpec as P

CAP = 32
AHEAD = 4
MESH = pl.DeviceIdType.MESH
def chunk_width(n):
    return 512 if n <= 4 else 1024


NT = (((1,), (1,)), ((), ()))
TN = (((0,), (0,)), ((), ()))


def kernel(
    n,
    n_sec,
    ids_ref,
    slots_ref,
    scale_ref,
    tok_hbm,
    cot_hbm,
    gw_hbm,
    uw_hbm,
    dw_hbm,
    next_hbm,
    prior_hbm,
    tok,
    cot,
    gw,
    uw,
    dw,
    rows_all,
    rs_in,
    fin,
    shift,
    route,
    route_in,
    gate,
    up,
    grad,
    hid,
    load_sem,
    ag_send,
    ag_recv,
    rs_send,
    rs_recv,
    fin_send,
    fin_recv,
    shift_send,
    shift_recv,
    route_send,
    route_recv,
    out_sem,
):
    f32, bf16 = jnp.float32, jnp.bfloat16
    sec = lax.axis_index("section")
    me = lax.axis_index("expert")
    d = tok.shape[1]
    ch = chunk_width(n)
    nc = d // ch
    has_right, has_left = me < n - 1, me > 0
    has_next, has_prev = sec < n_sec - 1, sec > 0
    right = (sec, jnp.minimum(me + 1, n - 1))
    left = (sec, jnp.maximum(me - 1, 0))
    after = (jnp.minimum(sec + 1, n_sec - 1), me)
    before = (jnp.maximum(sec - 1, 0), me)
    neighbours = ((has_right, right), (has_left, left), (has_next, after), (has_prev, before))

    loads = [
        pltpu.make_async_copy(src, dst, load_sem.at[k])
        for k, (src, dst) in enumerate(
            ((tok_hbm, tok), (cot_hbm, cot), (gw_hbm, gw), (uw_hbm, uw), (dw_hbm, dw))
        )
    ]
    for load in loads:
        load.start()

    barrier = pltpu.get_barrier_semaphore()
    for exists, where in neighbours:

        @pl.when(exists)
        def _():
            pl.semaphore_signal(barrier, inc=1, device_id=where, device_id_type=MESH)

    def col(c):
        return pl.ds(pl.multiple_of(c * ch, ch), ch)

    hit = ids_ref[...] == sec
    slot = jnp.sum(jnp.where(hit, slots_ref[...], 0), axis=0, keepdims=True)
    weight = jnp.sum(jnp.where(hit, scale_ref[...], 0.0), axis=0, keepdims=True)
    chosen = jnp.sum(hit.astype(jnp.int32), axis=0, keepdims=True)
    place = lax.broadcasted_iota(jnp.int32, (128, hit.shape[1]), 0)
    picks = jnp.where((place == slot) & (chosen > 0), 1.0, 0.0)
    route[...] = jnp.transpose(jnp.where(place < CAP, picks, weight))

    def gather_own(a):
        @pl.loop(0, nc)
        def _(c):
            table = route[:, :CAP].astype(bf16)
            if a == 0:
                rows = tok[:, col(c)]
            else:
                rows = (route[:, CAP : CAP + 1] * cot[:, col(c)].astype(f32)).astype(bf16)
            got = lax.dot_general(table, rows, TN, preferred_element_type=f32)
            rows_all[a, me, :, col(c)] = got.astype(bf16)

    def ag_copy(u, j, way):
        ref = rows_all.at[u // nc, j, :, col(u % nc)]
        return pltpu.make_async_remote_copy(
            src_ref=ref,
            dst_ref=ref,
            send_sem=ag_send.at[u, way, j],
            recv_sem=ag_recv.at[u, j],
            device_id=(right, left)[way],
            device_id_type=MESH,
        )

    def ag_own(u):
        for way in range(2):

            @pl.when((has_right, has_left)[way])
            def _():
                ag_copy(u, me, way).start()

    def ag_step(u, s):
        for way, j, ok in ((0, me - s, me - s >= 0), (1, me + s, me + s < n)):

            @pl.when(ok)
            def _():
                ag_copy(u, j, way).wait_recv()
                if s < n - 1:

                    @pl.when((has_right, has_left)[way])
                    def _():
                        ag_copy(u, j, way).start()

    def ag_sent(u):
        for s in range(n - 1):
            for way, j, ok in ((0, me - s, me - s >= 0), (1, me + s, me + s < n)):

                @pl.when(ok & (has_right, has_left)[way])
                def _():
                    ag_copy(u, j, way).wait_send()

    def rs_copy(a, j, c, way):
        into = j if way == 0 else jnp.where(j == me - 1, n, j)
        return pltpu.make_async_remote_copy(
            src_ref=rows_all.at[a, j, :, col(c)],
            dst_ref=rs_in.at[a, into, :, col(c)],
            send_sem=rs_send.at[a, j, c],
            recv_sem=rs_recv.at[a, into, c],
            device_id=(right, left)[way],
            device_id_type=MESH,
        )

    def rs_take(a, j, into, c):
        pltpu.make_async_remote_copy(
            src_ref=rows_all.at[a, j, :, col(c)],
            dst_ref=rs_in.at[a, into, :, col(c)],
            send_sem=rs_send.at[a, j, c],
            recv_sem=rs_recv.at[a, into, c],
            device_id=right,
            device_id_type=MESH,
        ).wait_recv()
        total = rows_all[a, j, :, col(c)].astype(f32) + rs_in[a, into, :, col(c)].astype(f32)
        rows_all[a, j, :, col(c)] = total.astype(bf16)

    def fin_copy(a, c):
        return pltpu.make_async_remote_copy(
            src_ref=rows_all.at[a, me, :, col(c)],
            dst_ref=fin.at[a, :, col(c)],
            send_sem=fin_send.at[a, c],
            recv_sem=fin_recv.at[a, c],
            device_id=(after, before)[a],
            device_id_type=MESH,
        )

    def rs_step(a, b):
        for way in range(2):
            c = b - (me, n - 1 - me)[way]
            into = (me, n)[way]
            has_in = (has_left, has_right)[way]

            @pl.when((c >= 0) & (c < nc))
            def _():
                for s in range(n - 1):
                    j = (n - 1 - s, s)[way]

                    @pl.when((j > me, j < me)[way])
                    def _():
                        @pl.when(has_in)
                        def _():
                            rs_take(a, j, j, c)

                        rs_copy(a, j, c, way).start()

                @pl.when(has_in)
                def _():
                    rs_take(a, me, into, c)

        c = b - (n - 1)

        @pl.when((c >= 0) & (c < nc) & (has_next, has_prev)[a])
        def _():
            fin_copy(a, c).start()

    def rs_sent(a, c):
        for j in range(n):
            for way, ok in ((0, j > me), (1, j < me)):

                @pl.when(ok)
                def _():
                    rs_copy(a, j, c, way).wait_send()

        @pl.when((has_next, has_prev)[a])
        def _():
            fin_copy(a, c).wait_send()

    def shift_copy(a):
        return pltpu.make_async_remote_copy(
            src_ref=(tok, cot)[a],
            dst_ref=shift.at[a],
            send_sem=shift_send.at[a],
            recv_sem=shift_recv.at[a],
            device_id=(after, before)[a],
            device_id_type=MESH,
        )

    def route_copy(a):
        return pltpu.make_async_remote_copy(
            src_ref=route,
            dst_ref=route_in.at[a],
            send_sem=route_send.at[a],
            recv_sem=route_recv.at[a],
            device_id=(after, before)[a],
            device_id_type=MESH,
        )

    def out_copy(a, c):
        return pltpu.make_async_copy(
            shift.at[a, :, col(c)], (next_hbm, prior_hbm)[a].at[:, col(c)], out_sem.at[a, c]
        )

    sends_on = (has_next, has_prev)
    takes_from = (has_prev, has_next)

    def finish(a, c):
        @pl.when(takes_from[a])
        def _():
            fin_copy(a, c).wait_recv()
            table = route_in[a, :, :CAP].astype(bf16)
            rows = jnp.dot(table, fin[a, :, col(c)], preferred_element_type=f32)
            if a == 0:
                rows = route_in[a, :, CAP : CAP + 1] * rows
            shift[a, :, col(c)] = (shift[a, :, col(c)].astype(f32) + rows).astype(bf16)

        @pl.when(jnp.logical_not(takes_from[a]))
        def _():
            shift[a, :, col(c)] = jnp.zeros((shift.shape[1], ch), bf16)

        out_copy(a, c).start()

    loads[0].wait()
    gather_own(0)
    peers = sum(exists.astype(jnp.int32) for exists, _w in neighbours)
    pl.semaphore_wait(barrier, peers)

    for u in range(AHEAD):
        ag_own(u)
    loads[1].wait()
    gather_own(1)
    for a in range(2):

        @pl.when(sends_on[a])
        def _():
            route_copy(a).start()
            shift_copy(a).start()

    m = n * CAP
    gate[...] = jnp.zeros_like(gate)
    up[...] = jnp.zeros_like(up)
    grad[...] = jnp.zeros_like(grad)

    @pl.loop(0, 2 * nc + n - 1)
    def _(t):
        @pl.when(t + AHEAD < 2 * nc)
        def _():
            ag_own(t + AHEAD)

        for s in range(1, n):

            @pl.when((t >= s) & (t - s < 2 * nc))
            def _():
                ag_step(t - s, s)

        c = t - (n - 1)
        b = c - nc

        @pl.when(c == 0)
        def _():
            loads[2].wait()
            loads[3].wait()

        @pl.when((c >= 0) & (b < 0))
        def _():
            rows = rows_all[0, :, :, col(c)].reshape(m, ch)
            gate[...] += jnp.dot(rows, gw[col(c), :], preferred_element_type=f32)
            up[...] += jnp.dot(rows, uw[col(c), :], preferred_element_type=f32)

        @pl.when(b == 0)
        def _():
            g = gate[...]
            hid[0] = (g * jax.nn.sigmoid(g) * up[...]).astype(bf16)
            loads[4].wait()

        @pl.when(b >= 0)
        def _():
            ag_sent(b)
            part = jnp.dot(hid[0], dw[:, col(b)], preferred_element_type=f32)
            rows_all[0, :, :, col(b)] = part.astype(bf16).reshape(n, CAP, ch)
            rs_step(0, b)
            rows = rows_all[1, :, :, col(b)].reshape(m, ch)
            grad[...] += lax.dot_general(rows, dw[:, col(b)], NT, preferred_element_type=f32)

    g = gate[...]
    sig = jax.nn.sigmoid(g)
    hid[0] = (grad[...] * (g * sig)).astype(bf16)
    hid[1] = (grad[...] * up[...] * (sig * (1.0 + g * (1.0 - sig)))).astype(bf16)

    for a in range(2):

        @pl.when(takes_from[a])
        def _():
            route_copy(a).wait_recv()
            shift_copy(a).wait_recv()

    @pl.loop(0, nc + n)
    def _(b):
        @pl.when(b < nc)
        def _():
            ag_sent(nc + b)
            part = lax.dot_general(hid[1], gw[col(b), :], NT, preferred_element_type=f32)
            part += lax.dot_general(hid[0], uw[col(b), :], NT, preferred_element_type=f32)
            rows_all[1, :, :, col(b)] = part.astype(bf16).reshape(n, CAP, ch)

        rs_step(0, nc + b)
        rs_step(1, b)

        @pl.when(b < nc)
        def _():
            finish(0, b)

        @pl.when(b >= n)
        def _():
            finish(1, b - n)

    for a in range(2):

        @pl.when(sends_on[a])
        def _():
            route_copy(a).wait_send()
            shift_copy(a).wait_send()

    @pl.loop(0, nc)
    def _(c):
        for a in range(2):
            rs_sent(a, c)
            out_copy(a, c).wait()


def body(
    n, n_sec, tokens, cotangent, expert_ids, slot_index, gate_scale, gate_weight, up_weight, down_weight
):
    t, d = tokens.shape[1:]
    h = gate_weight.shape[2]
    nc = d // chunk_width(n)
    m = n * CAP
    bf16, f32 = jnp.bfloat16, jnp.float32
    dma = pltpu.SemaphoreType.DMA
    vmem = pl.BlockSpec(memory_space=pltpu.VMEM)
    hbm = pl.BlockSpec(memory_space=pl.ANY)
    nxt, prior = pl.pallas_call(
        functools.partial(kernel, n, n_sec),
        out_shape=(jax.ShapeDtypeStruct((t, d), bf16), jax.ShapeDtypeStruct((t, d), bf16)),
        in_specs=[vmem] * 3 + [hbm] * 5,
        out_specs=(hbm, hbm),
        scratch_shapes=[
            pltpu.VMEM((t, d), bf16),
            pltpu.VMEM((t, d), bf16),
            pltpu.VMEM((d, h), bf16),
            pltpu.VMEM((d, h), bf16),
            pltpu.VMEM((h, d), bf16),
            pltpu.VMEM((2, n, CAP, d), bf16),
            pltpu.VMEM((2, n + 1, CAP, d), bf16),
            pltpu.VMEM((2, CAP, d), bf16),
            pltpu.VMEM((2, t, d), bf16),
            pltpu.VMEM((t, 128), f32),
            pltpu.VMEM((2, t, 128), f32),
            pltpu.VMEM((m, h), f32),
            pltpu.VMEM((m, h), f32),
            pltpu.VMEM((m, h), f32),
            pltpu.VMEM((2, m, h), bf16),
            dma((5,)),
            dma((2 * nc, 2, n)),
            dma((2 * nc, n)),
            dma((2, n, nc)),
            dma((2, n + 1, nc)),
            dma((2, nc)),
            dma((2, nc)),
            dma((2,)),
            dma((2,)),
            dma((2,)),
            dma((2,)),
            dma((2, nc)),
        ],
        compiler_params=pltpu.CompilerParams(
            collective_id=0, has_side_effects=True, vmem_limit_bytes=58 * 1024 * 1024
        ),
        cost_estimate=pl.CostEstimate(
            flops=12 * m * d * h, bytes_accessed=6 * d * h + 8 * t * d, transcendentals=0
        ),
    )(
        expert_ids[0].T,
        slot_index[0].T,
        gate_scale[0].T,
        tokens[0],
        cotangent[0],
        gate_weight[0],
        up_weight[0],
        down_weight[0],
    )
    return nxt[None], prior[None]


def solution(mesh):
    rows = P("section", "expert", None)
    in_specs = (rows,) * 5 + (P("section", None, "expert"),) * 2 + (rows,)
    return jax.shard_map(
        functools.partial(body, mesh.shape["expert"], mesh.shape["section"]),
        mesh=mesh,
        in_specs=in_specs,
        out_specs=(rows, rows),
        check_vma=False,
    )
```

```python
import functools

import jax
import jax.numpy as jnp
from jax import lax
from jax.experimental import pallas as pl
from jax.experimental.pallas import tpu as pltpu
from jax.sharding import PartitionSpec as P

CAP = 32
CH = 1024
AHEAD = 2
MESH = pl.DeviceIdType.MESH
NT = (((1,), (1,)), ((), ()))


def kernel(
    n,
    n_sec,
    sent_hbm,
    back_hbm,
    route,
    tok,
    cot,
    gw_hbm,
    uw_hbm,
    dw_hbm,
    shift0,
    shift1,
    route0,
    route1,
    fin0,
    fin1,
    gw,
    uw,
    dw,
    rows_all,
    rs_in,
    gate,
    up,
    grad,
    hid,
    load_sem,
    ag_send,
    ag_recv,
    rs_send,
    rs_recv,
    fin_send,
    fin_recv,
    shift_send,
    shift_recv,
    route_send,
    route_recv,
):
    f32, bf16 = jnp.float32, jnp.bfloat16
    sec = lax.axis_index("section")
    me = lax.axis_index("expert")
    d = gw.shape[0]
    nc = d // CH
    has_right, has_left = me < n - 1, me > 0
    has_next, has_prev = sec < n_sec - 1, sec > 0
    right = (sec, jnp.minimum(me + 1, n - 1))
    left = (sec, jnp.maximum(me - 1, 0))
    after = (jnp.minimum(sec + 1, n_sec - 1), me)
    before = (jnp.maximum(sec - 1, 0), me)
    neighbours = ((has_right, right), (has_left, left), (has_next, after), (has_prev, before))

    loads = [
        pltpu.make_async_copy(src, dst, load_sem.at[k])
        for k, (src, dst) in enumerate(
            (
                (sent_hbm, rows_all.at[0, me]),
                (back_hbm, rows_all.at[1, me]),
                (gw_hbm, gw),
                (uw_hbm, uw),
                (dw_hbm, dw),
            )
        )
    ]
    for load in loads:
        load.start()

    barrier = pltpu.get_barrier_semaphore()
    for exists, where in neighbours:

        @pl.when(exists)
        def _():
            pl.semaphore_signal(barrier, inc=1, device_id=where, device_id_type=MESH)

    def col(c):
        return pl.ds(pl.multiple_of(c * CH, CH), CH)

    def ag_copy(u, j, way):
        ref = rows_all.at[u // nc, j, :, col(u % nc)]
        return pltpu.make_async_remote_copy(
            src_ref=ref,
            dst_ref=ref,
            send_sem=ag_send.at[u, way, j],
            recv_sem=ag_recv.at[u, j],
            device_id=(right, left)[way],
            device_id_type=MESH,
        )

    def ag_own(u):
        for way in range(2):

            @pl.when((has_right, has_left)[way])
            def _():
                ag_copy(u, me, way).start()

    def ag_step(u, s):
        for way, j, ok in ((0, me - s, me - s >= 0), (1, me + s, me + s < n)):

            @pl.when(ok)
            def _():
                ag_copy(u, j, way).wait_recv()
                if s < n - 1:

                    @pl.when((has_right, has_left)[way])
                    def _():
                        ag_copy(u, j, way).start()

    def ag_sent(u):
        for s in range(n - 1):
            for way, j, ok in ((0, me - s, me - s >= 0), (1, me + s, me + s < n)):

                @pl.when(ok & (has_right, has_left)[way])
                def _():
                    ag_copy(u, j, way).wait_send()

    def rs_copy(a, j, c, way):
        into = j if way == 0 else jnp.where(j == me - 1, n, j)
        return pltpu.make_async_remote_copy(
            src_ref=rows_all.at[a, j, :, col(c)],
            dst_ref=rs_in.at[a, into, :, col(c)],
            send_sem=rs_send.at[a, j, c],
            recv_sem=rs_recv.at[a, into, c],
            device_id=(right, left)[way],
            device_id_type=MESH,
        )

    def rs_take(a, j, into, c):
        pltpu.make_async_remote_copy(
            src_ref=rows_all.at[a, j, :, col(c)],
            dst_ref=rs_in.at[a, into, :, col(c)],
            send_sem=rs_send.at[a, j, c],
            recv_sem=rs_recv.at[a, into, c],
            device_id=right,
            device_id_type=MESH,
        ).wait_recv()
        total = rows_all[a, j, :, col(c)].astype(f32) + rs_in[a, into, :, col(c)].astype(f32)
        rows_all[a, j, :, col(c)] = total.astype(bf16)

    def fin_copy(a, c):
        return pltpu.make_async_remote_copy(
            src_ref=rows_all.at[a, me, :, col(c)],
            dst_ref=(fin0, fin1)[a].at[:, col(c)],
            send_sem=fin_send.at[a, c],
            recv_sem=fin_recv.at[a, c],
            device_id=(after, before)[a],
            device_id_type=MESH,
        )

    def rs_step(a, b):
        for way in range(2):
            c = b - (me, n - 1 - me)[way]
            into = (me, n)[way]
            has_in = (has_left, has_right)[way]

            @pl.when((c >= 0) & (c < nc))
            def _():
                for s in range(n - 1):
                    j = (n - 1 - s, s)[way]

                    @pl.when((j > me, j < me)[way])
                    def _():
                        @pl.when(has_in)
                        def _():
                            rs_take(a, j, j, c)

                        rs_copy(a, j, c, way).start()

                @pl.when(has_in)
                def _():
                    rs_take(a, me, into, c)

        c = b - (n - 1)

        @pl.when((c >= 0) & (c < nc) & (has_next, has_prev)[a])
        def _():
            fin_copy(a, c).start()

    def rs_sent(a, c):
        for j in range(n):
            for way, ok in ((0, j > me), (1, j < me)):

                @pl.when(ok)
                def _():
                    rs_copy(a, j, c, way).wait_send()

        @pl.when((has_next, has_prev)[a])
        def _():
            fin_copy(a, c).wait_send()

    def shift_copy(a):
        return pltpu.make_async_remote_copy(
            src_ref=(tok, cot)[a],
            dst_ref=(shift0, shift1)[a],
            send_sem=shift_send.at[a],
            recv_sem=shift_recv.at[a],
            device_id=(after, before)[a],
            device_id_type=MESH,
        )

    def route_copy(a):
        return pltpu.make_async_remote_copy(
            src_ref=route,
            dst_ref=(route0, route1)[a],
            send_sem=route_send.at[a],
            recv_sem=route_recv.at[a],
            device_id=(after, before)[a],
            device_id_type=MESH,
        )

    sends_on = (has_next, has_prev)
    takes_from = (has_prev, has_next)

    loads[0].wait()
    loads[1].wait()
    peers = sum(exists.astype(jnp.int32) for exists, _w in neighbours)
    pl.semaphore_wait(barrier, peers)

    for u in range(AHEAD):
        ag_own(u)
    for a in range(2):

        @pl.when(sends_on[a])
        def _():
            route_copy(a).start()
            shift_copy(a).start()

    m = n * CAP
    gate[...] = jnp.zeros_like(gate)
    up[...] = jnp.zeros_like(up)
    grad[...] = jnp.zeros_like(grad)

    @pl.loop(0, 2 * nc + n - 1)
    def _(t):
        @pl.when(t + AHEAD < 2 * nc)
        def _():
            ag_own(t + AHEAD)

        for s in range(1, n):

            @pl.when((t >= s) & (t - s < 2 * nc))
            def _():
                ag_step(t - s, s)

        c = t - (n - 1)
        b = c - nc

        @pl.when(c == 0)
        def _():
            loads[2].wait()
            loads[3].wait()

        @pl.when((c >= 0) & (b < 0))
        def _():
            rows = rows_all[0, :, :, col(c)].reshape(m, CH)
            gate[...] += jnp.dot(rows, gw[col(c), :], preferred_element_type=f32)
            up[...] += jnp.dot(rows, uw[col(c), :], preferred_element_type=f32)

        @pl.when(b == 0)
        def _():
            g = gate[...]
            hid[0] = (g * jax.nn.sigmoid(g) * up[...]).astype(bf16)
            loads[4].wait()

        @pl.when(b >= 0)
        def _():
            ag_sent(b)
            part = jnp.dot(hid[0], dw[:, col(b)], preferred_element_type=f32)
            rows_all[0, :, :, col(b)] = part.astype(bf16).reshape(n, CAP, CH)
            rs_step(0, b)
            rows = rows_all[1, :, :, col(b)].reshape(m, CH)
            grad[...] += lax.dot_general(rows, dw[:, col(b)], NT, preferred_element_type=f32)

    g = gate[...]
    sig = jax.nn.sigmoid(g)
    hid[0] = (grad[...] * (g * sig)).astype(bf16)
    hid[1] = (grad[...] * up[...] * (sig * (1.0 + g * (1.0 - sig)))).astype(bf16)

    @pl.loop(0, nc + n - 1)
    def _(b):
        @pl.when(b < nc)
        def _():
            ag_sent(nc + b)
            part = lax.dot_general(hid[1], gw[col(b), :], NT, preferred_element_type=f32)
            part += lax.dot_general(hid[0], uw[col(b), :], NT, preferred_element_type=f32)
            rows_all[1, :, :, col(b)] = part.astype(bf16).reshape(n, CAP, CH)

        rs_step(0, nc + b)
        rs_step(1, b)

    for a in range(2):

        @pl.when(sends_on[a])
        def _():
            route_copy(a).wait_send()
            shift_copy(a).wait_send()

        @pl.when(takes_from[a])
        def _():
            route_copy(a).wait_recv()
            shift_copy(a).wait_recv()

    @pl.loop(0, nc)
    def _(c):
        for a in range(2):
            rs_sent(a, c)

            @pl.when(takes_from[a])
            def _():
                fin_copy(a, c).wait_recv()


def body(
    n, n_sec, tokens, cotangent, expert_ids, slot_index, gate_scale, gate_weight, up_weight, down_weight
):
    t, d = tokens.shape[1:]
    h = gate_weight.shape[2]
    nc = d // CH
    m = n * CAP
    bf16, f32 = jnp.bfloat16, jnp.float32
    dma = pltpu.SemaphoreType.DMA
    hbm = pl.BlockSpec(memory_space=pl.ANY)
    section = lax.axis_index("section")
    hit = expert_ids[0] == section
    slot = jnp.sum(jnp.where(hit, slot_index[0], 0), axis=1)
    weight = jnp.sum(jnp.where(hit, gate_scale[0], jnp.float32(0.0)), axis=1)
    place = jnp.where(jnp.any(hit, axis=1), slot, CAP)
    table = (jnp.arange(CAP, dtype=jnp.int32)[:, None] == place[None, :]).astype(bf16)
    sent = jnp.dot(table, tokens[0], preferred_element_type=f32).astype(bf16)
    carried = (weight[:, None] * cotangent[0].astype(f32)).astype(bf16)
    back = jnp.dot(table, carried, preferred_element_type=f32).astype(bf16)
    lane = jnp.arange(128, dtype=jnp.int32)[None, :]
    picks = (lane == place[:, None]).astype(f32)
    route = jnp.where(lane < CAP, picks, weight[:, None])
    shape = jax.ShapeDtypeStruct
    tok_in, cot_in, route0, route1, fin0, fin1 = pl.pallas_call(
        functools.partial(kernel, n, n_sec),
        out_shape=(shape((t, d), bf16),) * 2
        + (shape((t, 128), f32),) * 2
        + (shape((CAP, d), bf16),) * 2,
        in_specs=[hbm] * 8,
        out_specs=(hbm,) * 6,
        scratch_shapes=[
            pltpu.VMEM((d, h), bf16),
            pltpu.VMEM((d, h), bf16),
            pltpu.VMEM((h, d), bf16),
            pltpu.VMEM((2, n, CAP, d), bf16),
            pltpu.VMEM((2, n + 1, CAP, d), bf16),
            pltpu.VMEM((m, h), f32),
            pltpu.VMEM((m, h), f32),
            pltpu.VMEM((m, h), f32),
            pltpu.VMEM((2, m, h), bf16),
            dma((5,)),
            dma((2 * nc, 2, n)),
            dma((2 * nc, n)),
            dma((2, n, nc)),
            dma((2, n + 1, nc)),
            dma((2, nc)),
            dma((2, nc)),
            dma((2,)),
            dma((2,)),
            dma((2,)),
            dma((2,)),
        ],
        compiler_params=pltpu.CompilerParams(
            collective_id=0, has_side_effects=True, vmem_limit_bytes=58 * 1024 * 1024
        ),
        cost_estimate=pl.CostEstimate(
            flops=12 * m * d * h, bytes_accessed=6 * d * h + 8 * t * d, transcendentals=0
        ),
    )(
        sent,
        back,
        route,
        tokens[0],
        cotangent[0],
        gate_weight[0],
        up_weight[0],
        down_weight[0],
    )

    def place_rows(base, rows, source):
        got = jnp.dot(source[:, :CAP].astype(bf16), rows, preferred_element_type=f32)
        return base.astype(f32), got, source[:, CAP : CAP + 1]

    base, got, scale = place_rows(tok_in, fin0, route0)
    nxt = jnp.where(section > 0, base + scale * got, 0.0).astype(bf16)
    base, got, _ = place_rows(cot_in, fin1, route1)
    prior = jnp.where(section < n_sec - 1, base + got, 0.0).astype(bf16)
    return nxt[None], prior[None]


def solution(mesh):
    rows = P("section", "expert", None)
    in_specs = (rows,) * 5 + (P("section", None, "expert"),) * 2 + (rows,)
    return jax.shard_map(
        functools.partial(body, mesh.shape["expert"], mesh.shape["section"]),
        mesh=mesh,
        in_specs=in_specs,
        out_specs=(rows, rows),
        check_vma=False,
    )
```
